32 devices in a mesh: grp: 2 (over y), row: 16 (over z, x, core).
Axes of the slice: x: 2, y: 2, z: 4, core: 2. Of those that a mesh axis runs over, the one named last changes fastest.
Arguments:
- image: bfloat16 [128, 128, 3584], P(('grp', 'row')), parts along dimension 0, may hold values from -6 to 6
- mask: int32 [128, 2048], P(('grp', 'row')), parts along dimension 0, may hold values 0 or 1
- dictionary: bfloat16 [64, 4, 3584], replicated, may hold values from -0.046875 to 0.046875
- penalty: float32 [64], replicated, may hold values from 0.1 to 1
Outputs:
- codes: float32 [128, 128, 64], P(('grp', 'row')), parts along dimension 0
- grad_dict: float32 [7168, 256], P(('grp', 'row')), parts along dimension 0
The draws below stay inside these ranges and needn't reach their ends.
There are 2 independent parts, one for each index of `grp`. The reference program is written for one: setup_inputs(seed, part) draws one part's arguments, and reference() takes and returns one part's arrays. A program takes and returns all parts, laid end to end along the dimension named above; an argument that names none is the same for every part. Nothing has to cross between parts.
All inputs are finite; a program needn't handle non-finite values. No bound on the sum of `mask` on one device may be relied on, other than what follows from the above.
Results may differ from the reference program's by a relative error of at most 0.0044.
Values may be sent and summed in bfloat16 or wider, within the bound.
A program may use at most 128 MiB of HBM per device.

```python
import math
import jax
import jax.numpy as jnp

BANDS = 224
ATOMS = 64
ITERS = 2
BC = 128
BR = 64


def with_ends(result, own_key, least, top_value):
    extent = result.shape
    spot = [jax.random.randint(jax.random.fold_in(own_key, axis), (), 0, extent[axis]) for axis in range(len(extent))]
    result = result.at[tuple(spot)].set(least)
    longest = extent.index(max(extent))
    spot[longest] = (spot[longest] + 1) % extent[longest]
    return result.at[tuple(spot)].set(top_value)


def spiked(values, rng, source, target, shards_of, factor):
    def block_of(dim):
        return (jnp.arange(values.shape[dim]) // (values.shape[dim] // shards_of)).reshape((-1,) + (1,) * (values.ndim - 1 - dim))

    one_side = jax.random.permutation(rng, shards_of)[block_of(target)]
    second = (block_of(target) + shards_of // 2) % shards_of
    return jnp.where((block_of(source) == one_side) | (block_of(source) == second), factor * values, values)


def levels(own_key, extent, split, least, high):
    loudness = 1.0
    for dim, blocks in split:
        steps = jax.random.uniform(jax.random.fold_in(jax.random.fold_in(own_key, 6), dim), (blocks,), jnp.float32, least / len(split), high / len(split))
        loudness = loudness * jnp.repeat(jnp.exp(steps), extent[dim] // blocks).reshape((-1,) + (1,) * (len(extent) - 1 - dim))
    return loudness


def bell_draw(own_key, extent, spread, reach, cuts=(), held_as=jnp.bfloat16):
    drawn = jax.random.normal(own_key, extent, jnp.float32) * spread
    if len(cuts) > 0:
        drawn = levels(own_key, extent, cuts, -0.22, 0.18) * drawn
    return jnp.clip(drawn, min=-reach, max=reach).astype(held_as)


def heavy_noise(own_key, dims, scale, most, cuts, heavy, held_as=jnp.bfloat16):
    entries = scale * jax.random.normal(own_key, dims, jnp.float32)
    if cuts:
        entries = entries * levels(own_key, dims, cuts, -0.22, 0.18)
    return jnp.clip(spiked(entries, jax.random.fold_in(own_key, 3), *heavy), -most, most).astype(held_as)


def setup_inputs(seed: int = 0, part: int = 0) -> dict:
    keys = jax.random.split(jax.random.key(seed), 5)
    part_splits = jax.random.split(jax.random.fold_in(keys[4], part), 5)
    return {
        "image": heavy_noise(part_splits[0], (BR, BC, 16 * BANDS), 1.0, 6.0, ((0, 16),), (0, 2, 16, 2.0)),
        "mask": with_ends((jax.random.randint(part_splits[1], (BR, BC * 16), 0, 4) < 3).astype(jnp.int32), jax.random.fold_in(part_splits[1], 1), 0, 1),
        "dictionary": bell_draw(keys[2], (ATOMS, 4, 16 * BANDS), (64 * BANDS) ** -0.5, 0.046875),
        "penalty": jnp.clip(jnp.exp(jax.random.uniform(keys[3], (ATOMS,), jnp.float32, math.log(0.1), math.log(1.0))), 0.1, 1.0),
    }


STEP_SIZE = 0.5

def shift_down_right(values, row_off, col_off):
    padded = jnp.pad(values, ((row_off, 0), (col_off, 0), (0, 0)))
    return padded[:values.shape[0], :values.shape[1]]

def shift_up_left(values, row_off, col_off):
    padded = jnp.pad(values, ((0, row_off), (0, col_off), (0, 0)))
    return padded[row_off:, col_off:]

def synthesize(coded, dictionary):
    total = jnp.zeros((BR, BC, 16 * BANDS), jnp.float32)
    flat = coded.reshape(BR * BC, ATOMS)
    for row_off in range(2):
        for col_off in range(2):
            term = jnp.dot(flat, dictionary[:, 2 * row_off + col_off], preferred_element_type=jnp.float32)
            total = total + shift_down_right(term.reshape(BR, BC, 16 * BANDS), row_off, col_off)
    return total

def correlate(resid, dictionary):
    flat = resid.reshape(BR * BC, 16 * BANDS)
    total = jnp.zeros((BR, BC, ATOMS), jnp.float32)
    for row_off in range(2):
        for col_off in range(2):
            term = jnp.dot(flat, dictionary[:, 2 * row_off + col_off].T, preferred_element_type=jnp.float32)
            total = total + shift_up_left(term.reshape(BR, BC, ATOMS), row_off, col_off)
    return total

def residual_of(image, weight, coded, dictionary):
    approx = synthesize(coded, dictionary)
    diff = (image.astype(jnp.float32) - approx).reshape(BR, BC, 16, BANDS)
    return (weight * diff).reshape(BR, BC, 16 * BANDS).astype(jnp.bfloat16)

def shrink(values, limit):
    return values - jnp.clip(values, -limit, limit)

def reference(image, mask, dictionary, penalty):
    weight = mask.reshape(BR, BC, 16, 1).astype(jnp.float32)
    limit = STEP_SIZE * penalty
    start = (weight * image.astype(jnp.float32).reshape(BR, BC, 16, BANDS)).reshape(BR, BC, 16 * BANDS).astype(jnp.bfloat16)
    codes = shrink(STEP_SIZE * correlate(start, dictionary), limit)
    for sweep in range(ITERS - 1):
        resid = residual_of(image, weight, codes.astype(jnp.bfloat16), dictionary)
        codes = shrink(codes + STEP_SIZE * correlate(resid, dictionary), limit)
    rounded = codes.astype(jnp.bfloat16)
    resid = residual_of(image, weight, rounded, dictionary)
    flat = resid.reshape(BR * BC, 16 * BANDS)
    pieces = []
    for row_off in range(2):
        for col_off in range(2):
            moved = shift_down_right(rounded, row_off, col_off).reshape(BR * BC, ATOMS)
            pieces.append(jnp.dot(flat.T, moved, preferred_element_type=jnp.float32))
    scale = -1.0 / math.sqrt(BR * BC)
    grad_dict = jnp.concatenate(pieces, axis=1) * scale
    return (codes, grad_dict)
```

```python
import functools
import math

import jax
import jax.numpy as jnp
from jax import lax
from jax.experimental import pallas as pl
from jax.experimental.pallas import tpu as pltpu
from jax.sharding import PartitionSpec as P

STEP_SIZE = 0.5
QUAD = 4
F32 = jnp.float32
BF16 = jnp.bfloat16


def chunk_of(step, mine, quads):
    if quads == 4:
        return (3 - mine, (mine + 2) % 4, mine + 1 - 2 * (mine % 2), mine)[step]
    return (mine + 1 + step) % quads


def kernel(
    devices, block_rows, columns, fused,
    image_hbm, mask_ref, dict_hbm, penalty_ref,
    codes_ref, grad_ref,
    img, dic, weight, resid, spread, totals, low_out, low_in, wide, wide_in,
    partial, core_out, core_in, side_out, side_in, far_out, far_in,
    image_sem, dict_sem, low_send, low_recv, wide_send, wide_recv,
    core_send, core_recv, side_send, side_recv, far_send, far_recv,
):
    grp = lax.axis_index("grp")
    me = lax.axis_index("row")
    total_rows, features = img.shape
    bands = features // 16
    scale = -1.0 / math.sqrt(block_rows * devices * columns)
    quads = devices // QUAD
    core, side, far = me % 2, (me // 2) % 2, me // QUAD
    sibling = me + 1 - 2 * core
    beside = me + 2 - 4 * side
    first, last = slice(0, columns), slice(total_rows - columns, total_rows)

    def to(index):
        return dict(device_id=(grp, index), device_id_type=pl.DeviceIdType.MESH)

    barrier = pltpu.get_barrier_semaphore()

    @pl.when(me > 0)
    def _():
        pl.semaphore_signal(barrier, inc=1, **to(me - 1))

    @pl.when(me < devices - 1)
    def _():
        pl.semaphore_signal(barrier, inc=1, **to(me + 1))

    if fused:
        pl.semaphore_signal(barrier, inc=1, **to(beside))
        for step in range(quads - 1):
            other = chunk_of(step, far, quads) * QUAD + 2 * side + core
            pl.semaphore_signal(barrier, inc=1, **to(other))

    load_dict = pltpu.make_async_copy(dict_hbm, dic, dict_sem)
    load_image = pltpu.make_async_copy(image_hbm, img, image_sem)
    load_image.start()
    load_dict.start()

    @pl.when(me == 0)
    def _():
        wide_in[...] = jnp.zeros_like(wide_in)

    @pl.when(me == devices - 1)
    def _():
        low_in[...] = jnp.zeros_like(low_in)

    lane = lax.broadcasted_iota(jnp.int32, (8, 128), 1) // 16
    keep = lane == lax.broadcasted_iota(jnp.int32, (8, 128), 0)
    for i in range(block_rows):
        for j in range(columns // 8):
            flags = mask_ref[i : i + 1, j * 128 : (j + 1) * 128].astype(F32)
            spread[i * columns + j * 8 : i * columns + (j + 1) * 8, :] = jnp.where(
                keep, jnp.broadcast_to(flags, (8, 128)), 0.0
            )
    load_image.wait()

    width = 512 if features % 512 == 0 else 128

    def cut(index, size):
        return pl.ds(pl.multiple_of(index * size, 128), size)

    def start_chunk(index, carry):
        here = cut(index, width)
        place = lax.broadcasted_iota(jnp.int32, (128, width), 1) + index * width
        begin = (lax.broadcasted_iota(jnp.int32, (128, width), 0) % 16) * bands
        inside = (place >= begin) & (place < begin + bands)
        expand = jnp.where(inside, 1.0, 0.0).astype(BF16)
        spots = jnp.dot(spread[...].astype(BF16), expand, preferred_element_type=F32)
        spots = spots.astype(BF16)
        weight[:, here] = spots
        resid[:, here] = img[:, here] * spots
        return carry

    lax.fori_loop(0, features // width, start_chunk, 0)
    load_dict.wait()
    above = (me + devices - 1) // devices
    below = (2 * devices - 2 - me) // devices
    pl.semaphore_wait(barrier, above + below + (quads if fused else 0))

    limit = STEP_SIZE * penalty_ref[...]

    def scores(rows):
        return lax.dot_general(
            resid[rows, :], dic[...], (((1,), (1,)), ((), ())), preferred_element_type=F32
        )

    def low_copy(sweep):
        return pltpu.make_async_remote_copy(
            low_out.at[sweep], low_in.at[sweep], low_send.at[sweep], low_recv.at[sweep], **to(me - 1)
        )

    def wide_copy(sweep):
        return pltpu.make_async_remote_copy(
            wide.at[sweep, last], wide_in.at[sweep], wide_send.at[sweep], wide_recv.at[sweep], **to(me + 1)
        )

    def update(sweep, rows, sums):
        count = sums.shape[0]
        column = lax.broadcasted_iota(jnp.int32, (count, 128), 0) % columns
        moved = jnp.where(column == columns - 1, 0.0, pltpu.roll(sums, count - 1, 0))
        found = STEP_SIZE * (sums[:, :64] + moved[:, 64:])
        if sweep > 0:
            found = codes_ref[rows, :] + found
        found = found - jnp.clip(found, -limit, limit)
        codes_ref[rows, :] = found
        both = jnp.concatenate([found, found], axis=1)
        shifted = jnp.where(column == 0, 0.0, pltpu.roll(both, 1, 0))
        half = lax.broadcasted_iota(jnp.int32, (count, 128), 1) < 64
        wide[sweep, rows, :] = jnp.where(half, both, shifted).astype(BF16)

    def analyze(sweep):
        found = scores(first)
        low_out[sweep] = found[:, 128:]

        @pl.when(me > 0)
        def _():
            low_copy(sweep).start()

        totals[first, :] = found[:, :128]
        rest = scores(slice(columns, total_rows))
        totals[columns:, :] = rest[:, :128]
        upto = total_rows - columns
        update(sweep, slice(0, upto), totals[:upto, :] + rest[:, 128:])

        @pl.when(me < devices - 1)
        def _():
            low_copy(sweep).wait_recv()

        update(sweep, last, totals[last, :] + low_in[sweep])

        @pl.when(me < devices - 1)
        def _():
            wide_copy(sweep).start()

    def fold(sweep, which):
        if which == "rest":
            return jnp.concatenate(
                [wide[sweep, columns:, :], wide[sweep, : total_rows - columns, :]], axis=1
            )
        return jnp.concatenate([wide[sweep, first, :], wide_in[sweep]], axis=1)

    def residual(sweep, rows, which, here):
        approx = jnp.dot(fold(sweep, which), dic[:, here], preferred_element_type=F32)
        diff = img[rows, here].astype(F32) - approx
        resid[rows, here] = diff.astype(BF16) * weight[rows, here]

    analyze(0)

    def rest_chunk(index, carry):
        residual(0, slice(columns, total_rows), "rest", cut(index, width))
        return carry

    def first_chunk(index, carry):
        residual(0, first, "first", cut(index, width))
        return carry

    def await_above(sweep):
        @pl.when(me > 0)
        def _():
            wide_copy(sweep).wait_recv()

    lax.fori_loop(0, features // width, rest_chunk, 0)
    await_above(0)
    lax.fori_loop(0, features // width, first_chunk, 0)
    analyze(1)

    chunk = features // quads if fused else features // 4
    own = chunk // QUAD

    def gradient(here):
        residual(1, slice(columns, total_rows), "rest", here)
        residual(1, first, "first", here)
        codes = jnp.concatenate([fold(1, "first"), fold(1, "rest")], axis=0)
        found = lax.dot_general(
            resid[:, here], codes, (((0,), (0,)), ((), ())), preferred_element_type=F32
        )
        return found * scale

    await_above(1)
    if not fused:
        for step in range(4):
            grad_ref[step * chunk : (step + 1) * chunk, :] = gradient(cut(step, chunk))
    else:
        def piece(step, index):
            return partial[step, pl.ds(pl.multiple_of(index * own, 16), own), :]

        def core_copy(step):
            return pltpu.make_async_remote_copy(
                core_out.at[step], core_in.at[step], core_send.at[step], core_recv.at[step], **to(sibling)
            )

        def side_copy(step):
            return pltpu.make_async_remote_copy(
                side_out.at[step], side_in.at[step], side_send.at[step], side_recv.at[step], **to(beside)
            )

        def far_copy(step):
            owner = chunk_of(step, far, quads) * QUAD + 2 * side + core
            return pltpu.make_async_remote_copy(
                far_out.at[step], far_in.at[step], far_send.at[step], far_recv.at[step], **to(owner)
            )

        def stage_core(step):
            partial[step] = gradient(cut(chunk_of(step, far, quads), chunk))
            for across in range(2):
                core_out[step, across] = piece(step, 2 * across + 1 - core).astype(BF16)
            core_copy(step).start()

        def stage_side(step):
            core_copy(step).wait_recv()
            across = 1 - side
            side_out[step] = (piece(step, 2 * across + core) + core_in[step, across].astype(F32)).astype(BF16)
            side_copy(step).start()

        def summed(step):
            side_copy(step).wait_recv()
            mine = piece(step, 2 * side + core) + core_in[step, side].astype(F32)
            return mine + side_in[step].astype(F32)

        def stage_far(step):
            far_out[step] = summed(step).astype(BF16)
            far_copy(step).start()

        for step in range(quads):
            stage_core(step)
            if step >= 1:
                stage_side(step - 1)
            if step >= 2:
                stage_far(step - 2)
        stage_side(quads - 1)
        if quads >= 2:
            stage_far(quads - 2)
        result = summed(quads - 1)
        for step in range(quads - 1):
            far_copy(step).wait_recv()
            result = result + far_in[step].astype(F32)
        grad_ref[...] = result
        for step in range(quads):
            core_copy(step).wait_send()
            side_copy(step).wait_send()
            if step < quads - 1:
                far_copy(step).wait_send()

    for sweep in range(2):
        @pl.when(me > 0)
        def _():
            low_copy(sweep).wait_send()

        @pl.when(me < devices - 1)
        def _():
            wide_copy(sweep).wait_send()


def local(devices, image, mask, dictionary, penalty):
    block_rows, columns, features = image.shape
    atoms = dictionary.shape[0]
    rows = block_rows * columns
    quads = devices // QUAD
    fused = devices % QUAD == 0 and features % (quads * 128) == 0 and features // devices % 16 == 0
    own = features // devices
    slots = (quads, own) if fused else (1, 16)
    flat = jnp.transpose(dictionary, (1, 0, 2)).reshape(4 * atoms, features)
    dma, vmem = pltpu.SemaphoreType.DMA, pltpu.VMEM
    near, there = pl.BlockSpec(memory_space=pltpu.VMEM), pl.BlockSpec(memory_space=pl.ANY)
    codes, grad = pl.pallas_call(
        functools.partial(kernel, devices, block_rows, columns, fused),
        out_shape=(
            jax.ShapeDtypeStruct((rows, atoms), F32),
            jax.ShapeDtypeStruct((own if fused else features, 4 * atoms), F32),
        ),
        in_specs=[there, near, there, near],
        out_specs=(near, near),
        scratch_shapes=[
            vmem((rows, features), BF16),
            vmem((4 * atoms, features), BF16),
            vmem((rows, features), BF16),
            vmem((rows, features), BF16),
            vmem((rows, 128), F32),
            vmem((rows, 128), F32),
            vmem((2, columns, 128), F32),
            vmem((2, columns, 128), F32),
            vmem((2, rows, 128), BF16),
            vmem((2, columns, 128), BF16),
            vmem((slots[0], QUAD * slots[1], 4 * atoms), F32),
            vmem((slots[0], 2, slots[1], 4 * atoms), BF16),
            vmem((slots[0], 2, slots[1], 4 * atoms), BF16),
            vmem((slots[0], slots[1], 4 * atoms), BF16),
            vmem((slots[0], slots[1], 4 * atoms), BF16),
            vmem((slots[0], slots[1], 4 * atoms), BF16),
            vmem((slots[0], slots[1], 4 * atoms), BF16),
            dma, dma,
            dma((2,)), dma((2,)), dma((2,)), dma((2,)),
            dma((slots[0],)), dma((slots[0],)), dma((slots[0],)),
            dma((slots[0],)), dma((slots[0],)), dma((slots[0],)),
        ],
        compiler_params=pltpu.CompilerParams(
            collective_id=0, has_side_effects=True, vmem_limit_bytes=56 * 1024 * 1024
        ),
    )(image.reshape(rows, features), mask, flat, penalty.reshape(1, atoms))
    if not fused:
        grad = lax.psum_scatter(grad, "row", scatter_dimension=0, tiled=True)
    return (codes.reshape(block_rows, columns, atoms), grad)


def solution(mesh):
    return jax.shard_map(
        functools.partial(local, mesh.shape["row"]),
        mesh=mesh,
        in_specs=(P(("grp", "row"), None, None), P(("grp", "row"), None), P(), P()),
        out_specs=(P(("grp", "row"), None, None), P(("grp", "row"), None)),
        check_vma=False,
    )
```

```python
import functools
import math

import jax
import jax.numpy as jnp
from jax import lax
from jax.experimental import pallas as pl
from jax.experimental.pallas import tpu as pltpu
from jax.sharding import PartitionSpec as P

STEP_SIZE = 0.5
QUAD = 4
F32 = jnp.float32
BF16 = jnp.bfloat16


def chunk_of(step, mine, quads):
    if quads == 4:
        return (3 - mine, (mine + 2) % 4, mine + 1 - 2 * (mine % 2), mine)[step]
    return (mine + 1 + step) % quads


def target_of(step, mine, quads):
    return chunk_of(2 if quads == 4 and step == 0 else step, mine, quads)


def kernel(
    devices, block_rows, columns, fused,
    image_hbm, mask_ref, dict_hbm, penalty_ref,
    codes_out, grad_ref,
    codes_ref, raw, img, dic, weight, resid, spread, totals, low_out, low_in, wide, wide_in,
    partial, core_out, core_in, side_out, side_in, far_out, far_in,
    image_sem, dict_sem, low_send, low_recv, wide_send, wide_recv,
    core_send, core_recv, side_send, side_recv, far_send, far_recv,
):
    grp = lax.axis_index("grp")
    me = lax.axis_index("row")
    total_rows, features = img.shape
    bands = features // 16
    scale = -1.0 / math.sqrt(block_rows * devices * columns)
    quads = devices // QUAD
    core, side, far = me % 2, (me // 2) % 2, me // QUAD
    sibling = me + 1 - 2 * core
    beside = me + 2 - 4 * side
    first, last = slice(0, columns), slice(total_rows - columns, total_rows)

    def to(index):
        return dict(device_id=(grp, index), device_id_type=pl.DeviceIdType.MESH)

    barrier = pltpu.get_barrier_semaphore()

    @pl.when(me > 0)
    def _():
        pl.semaphore_signal(barrier, inc=1, **to(me - 1))

    @pl.when(me < devices - 1)
    def _():
        pl.semaphore_signal(barrier, inc=1, **to(me + 1))

    if fused:
        pl.semaphore_signal(barrier, inc=1, **to(beside))
        for step in range(1 if quads == 4 else 0, quads - 1):
            other = chunk_of(step, far, quads) * QUAD + 2 * side + core
            pl.semaphore_signal(barrier, inc=1, **to(other))

    peers = 3 if quads == 4 else quads
    load_dict = pltpu.make_async_copy(dict_hbm, raw, dict_sem)
    load_first = pltpu.make_async_copy(
        image_hbm.at[pl.ds(0, columns)], img.at[pl.ds(0, columns)], image_sem.at[0]
    )
    others = pl.ds(columns, total_rows - columns)
    load_rest = pltpu.make_async_copy(image_hbm.at[others], img.at[others], image_sem.at[1])
    load_dict.start()
    load_first.start()
    load_rest.start()

    @pl.when(me == 0)
    def _():
        wide_in[...] = jnp.zeros_like(wide_in)

    @pl.when(me == devices - 1)
    def _():
        low_in[...] = jnp.zeros_like(low_in)

    lane = lax.broadcasted_iota(jnp.int32, (8, 128), 1) // 16
    keep = lane == lax.broadcasted_iota(jnp.int32, (8, 128), 0)
    for i in range(block_rows):
        for j in range(columns // 8):
            flags = mask_ref[i : i + 1, j * 128 : (j + 1) * 128].astype(F32)
            spread[i * columns + j * 8 : i * columns + (j + 1) * 8, :] = jnp.where(
                keep, jnp.broadcast_to(flags, (8, 128)), 0.0
            )
    width = 512 if features % 512 == 0 else 128

    def cut(index, size):
        return pl.ds(pl.multiple_of(index * size, 128), size)

    def start_chunk(index, carry):
        here = cut(index, width)
        place = lax.broadcasted_iota(jnp.int32, (128, width), 1) + index * width
        begin = (lax.broadcasted_iota(jnp.int32, (128, width), 0) % 16) * bands
        inside = (place >= begin) & (place < begin + bands)
        picked = jnp.where(inside, 1.0, 0.0).astype(BF16)
        spots = jnp.dot(spread[...].astype(BF16), picked, preferred_element_type=F32)
        weight[:, here] = spots.astype(BF16)
        return carry

    lax.fori_loop(0, features // width, start_chunk, 0)
    load_dict.wait()
    atoms = raw.shape[0]
    for quarter in range(4):
        dic[quarter * atoms : (quarter + 1) * atoms, :] = raw[:, quarter, :]
    above = (me + devices - 1) // devices
    below = (2 * devices - 2 - me) // devices
    pl.semaphore_wait(barrier, above + below + (peers if fused else 0))

    limit = STEP_SIZE * penalty_ref[...]

    def scores(rows):
        return lax.dot_general(
            resid[rows, :], dic[...], (((1,), (1,)), ((), ())), preferred_element_type=F32
        )

    def low_copy(sweep):
        return pltpu.make_async_remote_copy(
            low_out.at[sweep], low_in.at[sweep], low_send.at[sweep], low_recv.at[sweep], **to(me - 1)
        )

    def wide_copy(sweep):
        return pltpu.make_async_remote_copy(
            wide.at[sweep, last], wide_in.at[sweep], wide_send.at[sweep], wide_recv.at[sweep], **to(me + 1)
        )

    def lift(values):
        count = values.shape[0]
        column = lax.broadcasted_iota(jnp.int32, values.shape, 0) % columns
        return jnp.where(column == columns - 1, 0.0, pltpu.roll(values, count - 1, 0))

    def update(sweep, rows, sums, extra=None):
        count = sums.shape[0]
        column = lax.broadcasted_iota(jnp.int32, (count, 128), 0) % columns
        found = sums[:, :64] + lift(sums)[:, 64:]
        if extra is not None:
            found = found + extra
        found = STEP_SIZE * found
        if sweep > 0:
            found = codes_ref[rows, :] + found
        found = found - jnp.clip(found, -limit, limit)
        if sweep == 0:
            codes_ref[rows, :] = found
        else:
            for i in range(count // columns):
                row = rows.start // columns + i
                codes_out[row] = found[i * columns : (i + 1) * columns, :].T
        both = jnp.concatenate([found, found], axis=1)
        shifted = jnp.where(column == 0, 0.0, pltpu.roll(both, 1, 0))
        half = lax.broadcasted_iota(jnp.int32, (count, 128), 1) < 64
        wide[sweep, rows, :] = jnp.where(half, both, shifted).astype(BF16)

    def analyze(sweep):
        if sweep == 0:
            load_first.wait()
            resid[first, :] = img[first, :] * weight[first, :]
        found = scores(first)
        below_row = found[:, 128:192] + lift(found[:, 128:])[:, 64:]
        half = columns // 2
        low_out[sweep] = jnp.concatenate([below_row[:half], below_row[half:]], axis=1)

        @pl.when(me > 0)
        def _():
            low_copy(sweep).start()

        totals[first, :] = found[:, :128]
        if sweep == 0:
            load_rest.wait()
            resid[columns:, :] = img[columns:, :] * weight[columns:, :]
        rest = scores(slice(columns, total_rows))
        totals[columns:, :] = rest[:, :128]
        upto = total_rows - columns
        update(sweep, slice(0, upto), totals[:upto, :] + rest[:, 128:])

        @pl.when(me < devices - 1)
        def _():
            low_copy(sweep).wait_recv()

        came = low_in[sweep]
        extra = jnp.concatenate([came[:, :64], came[:, 64:]], axis=0)
        update(sweep, last, totals[last, :], extra)

        @pl.when(me < devices - 1)
        def _():
            wide_copy(sweep).start()

    def fold(sweep, which):
        if which == "rest":
            return jnp.concatenate(
                [wide[sweep, columns:, :], wide[sweep, : total_rows - columns, :]], axis=1
            )
        return jnp.concatenate([wide[sweep, first, :], wide_in[sweep]], axis=1)

    def residual(sweep, rows, which, here):
        approx = jnp.dot(fold(sweep, which), dic[:, here], preferred_element_type=F32)
        diff = img[rows, here].astype(F32) - approx
        resid[rows, here] = diff.astype(BF16) * weight[rows, here]

    analyze(0)

    def rest_chunk(sweep, index, carry):
        residual(sweep, slice(columns, total_rows), "rest", cut(index, width))
        return carry

    def first_chunk(index, carry):
        residual(0, first, "first", cut(index, width))
        return carry

    def await_above(sweep):
        @pl.when(me > 0)
        def _():
            wide_copy(sweep).wait_recv()

    lax.fori_loop(0, features // width, functools.partial(rest_chunk, 0), 0)
    await_above(0)
    lax.fori_loop(0, features // width, first_chunk, 0)
    analyze(1)
    lax.fori_loop(0, features // width, functools.partial(rest_chunk, 1), 0)

    chunk = features // quads if fused else features // 4
    own = chunk // QUAD

    def gradient(here):
        residual(1, first, "first", here)
        codes = jnp.concatenate([fold(1, "first"), fold(1, "rest")], axis=0)
        found = lax.dot_general(
            resid[:, here], codes, (((0,), (0,)), ((), ())), preferred_element_type=F32
        )
        return found * scale

    await_above(1)
    if not fused:
        for step in range(4):
            grad_ref[step * chunk : (step + 1) * chunk, :] = gradient(cut(step, chunk))
    else:
        def piece(step, index):
            return partial[step, pl.ds(pl.multiple_of(index * own, 16), own), :]

        def core_copy(step):
            return pltpu.make_async_remote_copy(
                core_out.at[step], core_in.at[step], core_send.at[step], core_recv.at[step], **to(sibling)
            )

        def side_copy(step):
            return pltpu.make_async_remote_copy(
                side_out.at[step], side_in.at[step], side_send.at[step], side_recv.at[step], **to(beside)
            )

        def far_copy(step):
            owner = target_of(step, far, quads) * QUAD + 2 * side + core
            return pltpu.make_async_remote_copy(
                far_out.at[step], far_in.at[step], far_send.at[step], far_recv.at[step], **to(owner)
            )

        def stage_core(step):
            partial[step] = gradient(cut(chunk_of(step, far, quads), chunk))
            for across in range(2):
                core_out[step, across] = piece(step, 2 * across + 1 - core).astype(BF16)
            core_copy(step).start()

        def stage_side(step):
            core_copy(step).wait_recv()
            across = 1 - side
            side_out[step] = (piece(step, 2 * across + core) + core_in[step, across].astype(F32)).astype(BF16)
            side_copy(step).start()

        def summed(step):
            side_copy(step).wait_recv()
            mine = piece(step, 2 * side + core) + core_in[step, side].astype(F32)
            return mine + side_in[step].astype(F32)

        def stage_far(step):
            value = summed(step)
            if quads == 4 and step == 1:
                far_copy(0).wait_recv()
                value = value + far_in[0].astype(F32)
            far_out[step] = value.astype(BF16)
            far_copy(step).start()

        for step in range(quads):
            stage_core(step)
            if step >= 1:
                stage_side(step - 1)
            if step >= 2:
                stage_far(step - 2)
        stage_side(quads - 1)
        if quads >= 2:
            stage_far(quads - 2)
        result = summed(quads - 1)
        for step in range(1 if quads == 4 else 0, quads - 1):
            far_copy(step).wait_recv()
            result = result + far_in[step].astype(F32)
        grad_ref[...] = result
        for step in range(quads):
            core_copy(step).wait_send()
            side_copy(step).wait_send()
            if step < quads - 1:
                far_copy(step).wait_send()

    for sweep in range(2):
        @pl.when(me > 0)
        def _():
            low_copy(sweep).wait_send()

        @pl.when(me < devices - 1)
        def _():
            wide_copy(sweep).wait_send()


def hand_on(codes_in, grad_in, codes_out, grad_out, sems):
    moves = (
        pltpu.make_async_copy(codes_in, codes_out, sems.at[0]),
        pltpu.make_async_copy(grad_in, grad_out, sems.at[1]),
    )
    for move in moves:
        move.start()
    for move in moves:
        move.wait()


def local(devices, image, mask, dictionary, penalty):
    block_rows, columns, features = image.shape
    atoms = dictionary.shape[0]
    rows = block_rows * columns
    quads = devices // QUAD
    fused = devices % QUAD == 0 and features % (quads * 128) == 0 and features // devices % 16 == 0
    own = features // devices
    slots = (quads, own) if fused else (1, 16)
    dma, vmem = pltpu.SemaphoreType.DMA, pltpu.VMEM
    near, there = pl.BlockSpec(memory_space=pltpu.VMEM), pl.BlockSpec(memory_space=pl.ANY)
    codes, grad = pl.pallas_call(
        functools.partial(kernel, devices, block_rows, columns, fused),
        out_shape=(
            jax.ShapeDtypeStruct((block_rows, atoms, columns), F32),
            jax.ShapeDtypeStruct((own if fused else features, 4 * atoms), F32),
        ),
        in_specs=[there, near, there, near],
        out_specs=(near, near),
        scratch_shapes=[
            vmem((rows, atoms), F32),
            vmem((atoms, 4, features), BF16),
            vmem((rows, features), BF16),
            vmem((4 * atoms, features), BF16),
            vmem((rows, features), BF16),
            vmem((rows, features), BF16),
            vmem((rows, 128), F32),
            vmem((rows, 128), F32),
            vmem((2, columns // 2, 128), F32),
            vmem((2, columns // 2, 128), F32),
            vmem((2, rows, 128), BF16),
            vmem((2, columns, 128), BF16),
            vmem((slots[0], QUAD * slots[1], 4 * atoms), F32),
            vmem((slots[0], 2, slots[1], 4 * atoms), BF16),
            vmem((slots[0], 2, slots[1], 4 * atoms), BF16),
            vmem((slots[0], slots[1], 4 * atoms), BF16),
            vmem((slots[0], slots[1], 4 * atoms), BF16),
            vmem((slots[0], slots[1], 4 * atoms), BF16),
            vmem((slots[0], slots[1], 4 * atoms), BF16),
            dma((2,)), dma,
            dma((2,)), dma((2,)), dma((2,)), dma((2,)),
            dma((slots[0],)), dma((slots[0],)), dma((slots[0],)),
            dma((slots[0],)), dma((slots[0],)), dma((slots[0],)),
        ],
        compiler_params=pltpu.CompilerParams(
            collective_id=0, has_side_effects=True, vmem_limit_bytes=56 * 1024 * 1024
        ),
    )(image.reshape(rows, features), mask, dictionary, penalty.reshape(1, atoms))
    if not fused:
        grad = lax.psum_scatter(grad, "row", scatter_dimension=0, tiled=True)
    codes, grad = pl.pallas_call(
        hand_on,
        out_shape=(
            jax.ShapeDtypeStruct(codes.shape, F32),
            jax.ShapeDtypeStruct(grad.shape, F32),
        ),
        in_specs=[there, there],
        out_specs=(there, there),
        scratch_shapes=[dma((2,))],
    )(codes, grad)
    return (jnp.transpose(codes, (0, 2, 1)), grad)


def solution(mesh):
    return jax.shard_map(
        functools.partial(local, mesh.shape["row"]),
        mesh=mesh,
        in_specs=(P(("grp", "row"), None, None), P(("grp", "row"), None), P(), P()),
        out_specs=(P(("grp", "row"), None, None), P(("grp", "row"), None)),
        check_vma=False,
    )
```

```python
import functools
import math

import jax
import jax.numpy as jnp
from jax import lax
from jax.experimental import pallas as pl
from jax.experimental.pallas import tpu as pltpu
from jax.sharding import PartitionSpec as P

STEP_SIZE = 0.5
QUAD = 4
F32 = jnp.float32
BF16 = jnp.bfloat16


def chunk_of(step, mine, quads):
    if quads == 4:
        return (3 - mine, (mine + 2) % 4, mine + 1 - 2 * (mine % 2), mine)[step]
    return (mine + 1 + step) % quads


def target_of(step, mine, quads):
    return chunk_of(2 if quads == 4 and step == 0 else step, mine, quads)


def kernel(
    devices, block_rows, columns, fused,
    image_hbm, mask_ref, dict_hbm, penalty_ref,
    codes_out, grad_ref,
    codes_ref, raw, img, dic, weight, resid, spread, totals, low_out, low_in, wide, wide_in,
    partial, core_out, core_in, side_out, side_in, far_out, far_in,
    image_sem, dict_sem, low_send, low_recv, wide_send, wide_recv,
    core_send, core_recv, side_send, side_recv, far_send, far_recv,
):
    grp = lax.axis_index("grp")
    me = lax.axis_index("row")
    total_rows, features = img.shape
    bands = features // 16
    scale = -1.0 / math.sqrt(block_rows * devices * columns)
    quads = devices // QUAD
    core, side, far = me % 2, (me // 2) % 2, me // QUAD
    sibling = me + 1 - 2 * core
    beside = me + 2 - 4 * side
    first, last = slice(0, columns), slice(total_rows - columns, total_rows)

    def to(index):
        return dict(device_id=(grp, index), device_id_type=pl.DeviceIdType.MESH)

    barrier = pltpu.get_barrier_semaphore()

    @pl.when(me > 0)
    def _():
        pl.semaphore_signal(barrier, inc=1, **to(me - 1))

    @pl.when(me < devices - 1)
    def _():
        pl.semaphore_signal(barrier, inc=1, **to(me + 1))

    if fused:
        pl.semaphore_signal(barrier, inc=1, **to(beside))
        for step in range(1 if quads == 4 else 0, quads - 1):
            other = chunk_of(step, far, quads) * QUAD + 2 * side + core
            pl.semaphore_signal(barrier, inc=1, **to(other))

    peers = 3 if quads == 4 else quads
    load_dict = pltpu.make_async_copy(dict_hbm, raw, dict_sem)
    load_first = pltpu.make_async_copy(
        image_hbm.at[pl.ds(0, columns)], img.at[pl.ds(0, columns)], image_sem.at[0]
    )
    others = pl.ds(columns, total_rows - columns)
    load_rest = pltpu.make_async_copy(image_hbm.at[others], img.at[others], image_sem.at[1])
    load_dict.start()
    load_first.start()
    load_rest.start()

    @pl.when(me == 0)
    def _():
        wide_in[...] = jnp.zeros_like(wide_in)

    @pl.when(me == devices - 1)
    def _():
        low_in[...] = jnp.zeros_like(low_in)

    lane = lax.broadcasted_iota(jnp.int32, (8, 128), 1) // 16
    keep = lane == lax.broadcasted_iota(jnp.int32, (8, 128), 0)
    for i in range(block_rows):
        for j in range(columns // 8):
            flags = mask_ref[i : i + 1, j * 128 : (j + 1) * 128].astype(F32)
            spread[i * columns + j * 8 : i * columns + (j + 1) * 8, :] = jnp.where(
                keep, jnp.broadcast_to(flags, (8, 128)), 0.0
            )
    width = 512 if features % 512 == 0 else 128

    def cut(index, size):
        return pl.ds(pl.multiple_of(index * size, 128), size)

    def start_chunk(index, carry):
        here = cut(index, width)
        place = lax.broadcasted_iota(jnp.int32, (128, width), 1) + index * width
        begin = (lax.broadcasted_iota(jnp.int32, (128, width), 0) % 16) * bands
        inside = (place >= begin) & (place < begin + bands)
        picked = jnp.where(inside, 1.0, 0.0).astype(BF16)
        spots = jnp.dot(spread[...].astype(BF16), picked, preferred_element_type=F32)
        weight[:, here] = spots.astype(BF16)
        return carry

    lax.fori_loop(0, features // width, start_chunk, 0)
    load_dict.wait()
    atoms = raw.shape[0]
    dic[...] = jnp.swapaxes(raw[...], 0, 1).reshape(4 * atoms, features)
    above = (me + devices - 1) // devices
    below = (2 * devices - 2 - me) // devices
    pl.semaphore_wait(barrier, above + below + (peers if fused else 0))

    limit = STEP_SIZE * penalty_ref[...]

    def scores(rows):
        return lax.dot_general(
            resid[rows, :], dic[...], (((1,), (1,)), ((), ())), preferred_element_type=F32
        )

    def low_copy(sweep):
        return pltpu.make_async_remote_copy(
            low_out.at[sweep], low_in.at[sweep], low_send.at[sweep], low_recv.at[sweep], **to(me - 1)
        )

    def wide_copy(sweep):
        return pltpu.make_async_remote_copy(
            wide.at[sweep, last], wide_in.at[sweep], wide_send.at[sweep], wide_recv.at[sweep], **to(me + 1)
        )

    def lift(values):
        count = values.shape[0]
        column = lax.broadcasted_iota(jnp.int32, values.shape, 0) % columns
        return jnp.where(column == columns - 1, 0.0, pltpu.roll(values, count - 1, 0))

    def update(sweep, rows, sums, extra=None):
        count = sums.shape[0]
        column = lax.broadcasted_iota(jnp.int32, (count, 128), 0) % columns
        found = sums[:, :64] + lift(sums)[:, 64:]
        if extra is not None:
            found = found + extra
        found = STEP_SIZE * found
        if sweep > 0:
            found = codes_ref[rows, :] + found
        found = found - jnp.clip(found, -limit, limit)
        if sweep == 0:
            codes_ref[rows, :] = found
        else:
            for i in range(count // columns):
                row = rows.start // columns + i
                codes_out[row] = found[i * columns : (i + 1) * columns, :].T
        both = jnp.concatenate([found, found], axis=1)
        shifted = jnp.where(column == 0, 0.0, pltpu.roll(both, 1, 0))
        half = lax.broadcasted_iota(jnp.int32, (count, 128), 1) < 64
        wide[sweep, rows, :] = jnp.where(half, both, shifted).astype(BF16)

    def analyze(sweep):
        if sweep == 0:
            load_first.wait()
            resid[first, :] = img[first, :] * weight[first, :]
        found = scores(first)
        below_row = found[:, 128:192] + lift(found[:, 128:])[:, 64:]
        half = columns // 2
        low_out[sweep] = jnp.concatenate([below_row[:half], below_row[half:]], axis=1)

        @pl.when(me > 0)
        def _():
            low_copy(sweep).start()

        totals[first, :] = found[:, :128]
        if sweep == 0:
            load_rest.wait()
            resid[columns:, :] = img[columns:, :] * weight[columns:, :]
        rest = scores(slice(columns, total_rows))
        totals[columns:, :] = rest[:, :128]
        upto = total_rows - columns
        update(sweep, slice(0, upto), totals[:upto, :] + rest[:, 128:])

        @pl.when(me < devices - 1)
        def _():
            low_copy(sweep).wait_recv()

        came = low_in[sweep]
        extra = jnp.concatenate([came[:, :64], came[:, 64:]], axis=0)
        update(sweep, last, totals[last, :], extra)

        @pl.when(me < devices - 1)
        def _():
            wide_copy(sweep).start()

    def fold(sweep, which):
        if which == "rest":
            return jnp.concatenate(
                [wide[sweep, columns:, :], wide[sweep, : total_rows - columns, :]], axis=1
            )
        return jnp.concatenate([wide[sweep, first, :], wide_in[sweep]], axis=1)

    def residual(sweep, rows, which, here):
        approx = jnp.dot(fold(sweep, which), dic[:, here], preferred_element_type=F32)
        diff = img[rows, here].astype(F32) - approx
        resid[rows, here] = diff.astype(BF16) * weight[rows, here]

    analyze(0)

    def rest_chunk(sweep, index, carry):
        residual(sweep, slice(columns, total_rows), "rest", cut(index, width))
        return carry

    def first_chunk(index, carry):
        residual(0, first, "first", cut(index, width))
        return carry

    def await_above(sweep):
        @pl.when(me > 0)
        def _():
            wide_copy(sweep).wait_recv()

    lax.fori_loop(0, features // width, functools.partial(rest_chunk, 0), 0)
    await_above(0)
    lax.fori_loop(0, features // width, first_chunk, 0)
    analyze(1)
    lax.fori_loop(0, features // width, functools.partial(rest_chunk, 1), 0)

    chunk = features // quads if fused else features // 4
    own = chunk // QUAD

    def gradient(here):
        residual(1, first, "first", here)
        codes = jnp.concatenate([fold(1, "first"), fold(1, "rest")], axis=0)
        found = lax.dot_general(
            resid[:, here], codes, (((0,), (0,)), ((), ())), preferred_element_type=F32
        )
        return found * scale

    await_above(1)
    if not fused:
        for step in range(4):
            grad_ref[step * chunk : (step + 1) * chunk, :] = gradient(cut(step, chunk))
    else:
        def piece(step, index):
            return partial[step, pl.ds(pl.multiple_of(index * own, 16), own), :]

        def core_copy(step):
            return pltpu.make_async_remote_copy(
                core_out.at[step], core_in.at[step], core_send.at[step], core_recv.at[step], **to(sibling)
            )

        def side_copy(step):
            return pltpu.make_async_remote_copy(
                side_out.at[step], side_in.at[step], side_send.at[step], side_recv.at[step], **to(beside)
            )

        def far_copy(step):
            owner = target_of(step, far, quads) * QUAD + 2 * side + core
            return pltpu.make_async_remote_copy(
                far_out.at[step], far_in.at[step], far_send.at[step], far_recv.at[step], **to(owner)
            )

        def stage_core(step):
            partial[step] = gradient(cut(chunk_of(step, far, quads), chunk))
            for across in range(2):
                core_out[step, across] = piece(step, 2 * across + 1 - core).astype(BF16)
            core_copy(step).start()

        def stage_side(step):
            core_copy(step).wait_recv()
            across = 1 - side
            side_out[step] = (piece(step, 2 * across + core) + core_in[step, across].astype(F32)).astype(BF16)
            side_copy(step).start()

        def summed(step):
            side_copy(step).wait_recv()
            mine = piece(step, 2 * side + core) + core_in[step, side].astype(F32)
            return mine + side_in[step].astype(F32)

        def stage_far(step):
            value = summed(step)
            if quads == 4 and step == 1:
                far_copy(0).wait_recv()
                value = value + far_in[0].astype(F32)
            far_out[step] = value.astype(BF16)
            far_copy(step).start()

        for step in range(quads):
            stage_core(step)
            if step >= 1:
                stage_side(step - 1)
            if step >= 2:
                stage_far(step - 2)
        stage_side(quads - 1)
        if quads >= 2:
            stage_far(quads - 2)
        result = summed(quads - 1)
        for step in range(1 if quads == 4 else 0, quads - 1):
            far_copy(step).wait_recv()
            result = result + far_in[step].astype(F32)
        grad_ref[...] = result
        for step in range(quads):
            core_copy(step).wait_send()
            side_copy(step).wait_send()
            if step < quads - 1:
                far_copy(step).wait_send()

    for sweep in range(2):
        @pl.when(me > 0)
        def _():
            low_copy(sweep).wait_send()

        @pl.when(me < devices - 1)
        def _():
            wide_copy(sweep).wait_send()


def hand_on(codes_in, grad_in, codes_out, grad_out):
    codes_out[...] = codes_in[...]
    grad_out[...] = grad_in[...]


def local(devices, image, mask, dictionary, penalty):
    block_rows, columns, features = image.shape
    atoms = dictionary.shape[0]
    rows = block_rows * columns
    quads = devices // QUAD
    fused = devices % QUAD == 0 and features % (quads * 128) == 0 and features // devices % 16 == 0
    own = features // devices
    slots = (quads, own) if fused else (1, 16)
    dma, vmem = pltpu.SemaphoreType.DMA, pltpu.VMEM
    near, there = pl.BlockSpec(memory_space=pltpu.VMEM), pl.BlockSpec(memory_space=pl.ANY)
    codes, grad = pl.pallas_call(
        functools.partial(kernel, devices, block_rows, columns, fused),
        out_shape=(
            jax.ShapeDtypeStruct((block_rows, atoms, columns), F32),
            jax.ShapeDtypeStruct((own if fused else features, 4 * atoms), F32),
        ),
        in_specs=[there, near, there, near],
        out_specs=(near, near),
        scratch_shapes=[
            vmem((rows, atoms), F32),
            vmem((atoms, 4, features), BF16),
            vmem((rows, features), BF16),
            vmem((4 * atoms, features), BF16),
            vmem((rows, features), BF16),
            vmem((rows, features), BF16),
            vmem((rows, 128), F32),
            vmem((rows, 128), F32),
            vmem((2, columns // 2, 128), F32),
            vmem((2, columns // 2, 128), F32),
            vmem((2, rows, 128), BF16),
            vmem((2, columns, 128), BF16),
            vmem((slots[0], QUAD * slots[1], 4 * atoms), F32),
            vmem((slots[0], 2, slots[1], 4 * atoms), BF16),
            vmem((slots[0], 2, slots[1], 4 * atoms), BF16),
            vmem((slots[0], slots[1], 4 * atoms), BF16),
            vmem((slots[0], slots[1], 4 * atoms), BF16),
            vmem((slots[0], slots[1], 4 * atoms), BF16),
            vmem((slots[0], slots[1], 4 * atoms), BF16),
            dma((2,)), dma,
            dma((2,)), dma((2,)), dma((2,)), dma((2,)),
            dma((slots[0],)), dma((slots[0],)), dma((slots[0],)),
            dma((slots[0],)), dma((slots[0],)), dma((slots[0],)),
        ],
        compiler_params=pltpu.CompilerParams(
            collective_id=0, has_side_effects=True, vmem_limit_bytes=56 * 1024 * 1024
        ),
    )(image.reshape(rows, features), mask, dictionary, penalty.reshape(1, atoms))
    if not fused:
        grad = lax.psum_scatter(grad, "row", scatter_dimension=0, tiled=True)
    codes, grad = pl.pallas_call(
        hand_on,
        out_shape=(
            jax.ShapeDtypeStruct(codes.shape, F32),
            jax.ShapeDtypeStruct(grad.shape, F32),
        ),
        in_specs=[near, near],
        out_specs=(near, near),
    )(codes, grad)
    return (jnp.transpose(codes, (0, 2, 1)), grad)


def solution(mesh):
    return jax.shard_map(
        functools.partial(local, mesh.shape["row"]),
        mesh=mesh,
        in_specs=(P(("grp", "row"), None, None), P(("grp", "row"), None), P(), P()),
        out_specs=(P(("grp", "row"), None, None), P(("grp", "row"), None)),
        check_vma=False,
    )
```

```python
import functools
import math

import jax
import jax.numpy as jnp
from jax import lax
from jax.experimental import pallas as pl
from jax.experimental.pallas import tpu as pltpu
from jax.sharding import PartitionSpec as P

STEP_SIZE = 0.5
QUAD = 4
F32 = jnp.float32
BF16 = jnp.bfloat16


def chunk_of(step, mine, quads):
    if quads == 4:
        return (3 - mine, (mine + 2) % 4, mine + 1 - 2 * (mine % 2), mine)[step]
    return (mine + 1 + step) % quads


def target_of(step, mine, quads):
    return chunk_of(2 if quads == 4 and step == 0 else step, mine, quads)


def kernel(
    devices, block_rows, columns, fused,
    image_hbm, mask_ref, dict_hbm, penalty_ref,
    codes_out, grad_ref,
    codes_ref, raw, img, dic, weight, resid, spread, totals, low_out, low_in, wide, wide_in,
    partial, core_out, core_in, side_out, side_in, far_out, far_in,
    image_sem, dict_sem, low_send, low_recv, wide_send, wide_recv,
    core_send, core_recv, side_send, side_recv, far_send, far_recv,
):
    grp = lax.axis_index("grp")
    me = lax.axis_index("row")
    total_rows, features = img.shape
    bands = features // 16
    scale = -1.0 / math.sqrt(block_rows * devices * columns)
    quads = devices // QUAD
    core, side, far = me % 2, (me // 2) % 2, me // QUAD
    sibling = me + 1 - 2 * core
    beside = me + 2 - 4 * side
    first, last = slice(0, columns), slice(total_rows - columns, total_rows)

    def to(index):
        return dict(device_id=(grp, index), device_id_type=pl.DeviceIdType.MESH)

    barrier = pltpu.get_barrier_semaphore()

    @pl.when(me > 0)
    def _():
        pl.semaphore_signal(barrier, inc=1, **to(me - 1))

    @pl.when(me < devices - 1)
    def _():
        pl.semaphore_signal(barrier, inc=1, **to(me + 1))

    if fused:
        pl.semaphore_signal(barrier, inc=1, **to(beside))
        for step in range(1 if quads == 4 else 0, quads - 1):
            other = chunk_of(step, far, quads) * QUAD + 2 * side + core
            pl.semaphore_signal(barrier, inc=1, **to(other))

    peers = 3 if quads == 4 else quads
    load_dict = pltpu.make_async_copy(dict_hbm, raw, dict_sem)
    load_first = pltpu.make_async_copy(
        image_hbm.at[pl.ds(0, columns)], img.at[pl.ds(0, columns)], image_sem.at[0]
    )
    others = pl.ds(columns, total_rows - columns)
    load_rest = pltpu.make_async_copy(image_hbm.at[others], img.at[others], image_sem.at[1])
    load_dict.start()
    load_first.start()
    load_rest.start()

    @pl.when(me == 0)
    def _():
        wide_in[...] = jnp.zeros_like(wide_in)

    @pl.when(me == devices - 1)
    def _():
        low_in[...] = jnp.zeros_like(low_in)

    lane = lax.broadcasted_iota(jnp.int32, (8, 128), 1) // 16
    keep = lane == lax.broadcasted_iota(jnp.int32, (8, 128), 0)
    for i in range(block_rows):
        for j in range(columns // 8):
            flags = mask_ref[i : i + 1, j * 128 : (j + 1) * 128].astype(F32)
            spread[i * columns + j * 8 : i * columns + (j + 1) * 8, :] = jnp.where(
                keep, jnp.broadcast_to(flags, (8, 128)), 0.0
            )
    width = 512 if features % 512 == 0 else 128

    def cut(index, size):
        return pl.ds(pl.multiple_of(index * size, 128), size)

    def start_chunk(index, carry):
        here = cut(index, width)
        place = lax.broadcasted_iota(jnp.int32, (128, width), 1) + index * width
        begin = (lax.broadcasted_iota(jnp.int32, (128, width), 0) % 16) * bands
        inside = (place >= begin) & (place < begin + bands)
        picked = jnp.where(inside, 1.0, 0.0).astype(BF16)
        spots = jnp.dot(spread[...].astype(BF16), picked, preferred_element_type=F32)
        weight[:, here] = spots.astype(BF16)
        return carry

    lax.fori_loop(0, features // width, start_chunk, 0)
    load_dict.wait()
    atoms = raw.shape[0]
    dic[...] = jnp.swapaxes(raw[...], 0, 1).reshape(4 * atoms, features)
    above = (me + devices - 1) // devices
    below = (2 * devices - 2 - me) // devices
    pl.semaphore_wait(barrier, above + below + (peers if fused else 0))

    limit = STEP_SIZE * penalty_ref[...]

    def scores(rows):
        return lax.dot_general(
            resid[rows, :], dic[...], (((1,), (1,)), ((), ())), preferred_element_type=F32
        )

    def low_copy(sweep):
        return pltpu.make_async_remote_copy(
            low_out.at[sweep], low_in.at[sweep], low_send.at[sweep], low_recv.at[sweep], **to(me - 1)
        )

    def wide_copy(sweep):
        return pltpu.make_async_remote_copy(
            wide.at[sweep, last], wide_in.at[sweep], wide_send.at[sweep], wide_recv.at[sweep], **to(me + 1)
        )

    def lift(values):
        count = values.shape[0]
        column = lax.broadcasted_iota(jnp.int32, values.shape, 0) % columns
        return jnp.where(column == columns - 1, 0.0, pltpu.roll(values, count - 1, 0))

    def update(sweep, rows, sums, extra=None):
        count = sums.shape[0]
        column = lax.broadcasted_iota(jnp.int32, (count, 128), 0) % columns
        found = sums[:, :64] + lift(sums)[:, 64:]
        if extra is not None:
            found = found + extra
        found = STEP_SIZE * found
        if sweep > 0:
            found = codes_ref[rows, :] + found
        found = found - jnp.clip(found, -limit, limit)
        if sweep == 0:
            codes_ref[rows, :] = found
        else:
            for i in range(count // columns):
                row = rows.start // columns + i
                codes_out[row] = found[i * columns : (i + 1) * columns, :].T
        both = jnp.concatenate([found, found], axis=1)
        shifted = jnp.where(column == 0, 0.0, pltpu.roll(both, 1, 0))
        half = lax.broadcasted_iota(jnp.int32, (count, 128), 1) < 64
        wide[sweep, rows, :] = jnp.where(half, both, shifted).astype(BF16)

    def analyze(sweep):
        if sweep == 0:
            load_first.wait()
            resid[first, :] = img[first, :] * weight[first, :]
        found = scores(first)
        below_row = found[:, 128:192] + lift(found[:, 128:])[:, 64:]
        half = columns // 2
        low_out[sweep] = jnp.concatenate([below_row[:half], below_row[half:]], axis=1)

        @pl.when(me > 0)
        def _():
            low_copy(sweep).start()

        totals[first, :] = found[:, :128]
        if sweep == 0:
            load_rest.wait()
            resid[columns:, :] = img[columns:, :] * weight[columns:, :]
        rest = scores(slice(columns, total_rows))
        totals[columns:, :] = rest[:, :128]
        upto = total_rows - columns
        update(sweep, slice(0, upto), totals[:upto, :] + rest[:, 128:])

        @pl.when(me < devices - 1)
        def _():
            low_copy(sweep).wait_recv()

        came = low_in[sweep]
        extra = jnp.concatenate([came[:, :64], came[:, 64:]], axis=0)
        update(sweep, last, totals[last, :], extra)

        @pl.when(me < devices - 1)
        def _():
            wide_copy(sweep).start()

    def fold(sweep, which):
        if which == "rest":
            return jnp.concatenate(
                [wide[sweep, columns:, :], wide[sweep, : total_rows - columns, :]], axis=1
            )
        return jnp.concatenate([wide[sweep, first, :], wide_in[sweep]], axis=1)

    def residual(sweep, rows, which, here):
        approx = jnp.dot(fold(sweep, which), dic[:, here], preferred_element_type=F32)
        diff = img[rows, here].astype(F32) - approx
        resid[rows, here] = diff.astype(BF16) * weight[rows, here]

    analyze(0)

    def rest_chunk(sweep, index, carry):
        residual(sweep, slice(columns, total_rows), "rest", cut(index, width))
        return carry

    def first_chunk(index, carry):
        residual(0, first, "first", cut(index, width))
        return carry

    def await_above(sweep):
        @pl.when(me > 0)
        def _():
            wide_copy(sweep).wait_recv()

    lax.fori_loop(0, features // width, functools.partial(rest_chunk, 0), 0)
    await_above(0)
    lax.fori_loop(0, features // width, first_chunk, 0)
    analyze(1)
    lax.fori_loop(0, features // width, functools.partial(rest_chunk, 1), 0)

    chunk = features // quads if fused else features // 4
    own = chunk // QUAD

    def gradient(here):
        residual(1, first, "first", here)
        codes = jnp.concatenate([fold(1, "first"), fold(1, "rest")], axis=0)
        found = lax.dot_general(
            resid[:, here], codes, (((0,), (0,)), ((), ())), preferred_element_type=F32
        )
        return found * scale

    await_above(1)
    if not fused:
        for step in range(4):
            grad_ref[step * chunk : (step + 1) * chunk, :] = gradient(cut(step, chunk))
    else:
        def piece(step, index):
            return partial[step, pl.ds(pl.multiple_of(index * own, 16), own), :]

        def core_copy(step):
            return pltpu.make_async_remote_copy(
                core_out.at[step], core_in.at[step], core_send.at[step], core_recv.at[step], **to(sibling)
            )

        def side_copy(step):
            return pltpu.make_async_remote_copy(
                side_out.at[step], side_in.at[step], side_send.at[step], side_recv.at[step], **to(beside)
            )

        def far_copy(step):
            owner = target_of(step, far, quads) * QUAD + 2 * side + core
            return pltpu.make_async_remote_copy(
                far_out.at[step], far_in.at[step], far_send.at[step], far_recv.at[step], **to(owner)
            )

        def stage_core(step):
            partial[step] = gradient(cut(chunk_of(step, far, quads), chunk))
            for across in range(2):
                core_out[step, across] = piece(step, 2 * across + 1 - core).astype(BF16)
            core_copy(step).start()

        def stage_side(step):
            core_copy(step).wait_recv()
            across = 1 - side
            side_out[step] = (piece(step, 2 * across + core) + core_in[step, across].astype(F32)).astype(BF16)
            side_copy(step).start()

        def summed(step):
            side_copy(step).wait_recv()
            mine = piece(step, 2 * side + core) + core_in[step, side].astype(F32)
            return mine + side_in[step].astype(F32)

        def stage_far(step):
            value = summed(step)
            if quads == 4 and step == 1:
                far_copy(0).wait_recv()
                value = value + far_in[0].astype(F32)
            far_out[step] = value.astype(BF16)
            far_copy(step).start()

        for step in range(quads):
            stage_core(step)
            if step >= 1:
                stage_side(step - 1)
        stage_side(quads - 1)
        for step in range(quads - 1):
            stage_far(step)
        result = summed(quads - 1)
        for step in range(1 if quads == 4 else 0, quads - 1):
            far_copy(step).wait_recv()
            result = result + far_in[step].astype(F32)
        grad_ref[...] = result
        for step in range(quads):
            core_copy(step).wait_send()
            side_copy(step).wait_send()
            if step < quads - 1:
                far_copy(step).wait_send()

    for sweep in range(2):
        @pl.when(me > 0)
        def _():
            low_copy(sweep).wait_send()

        @pl.when(me < devices - 1)
        def _():
            wide_copy(sweep).wait_send()


def hand_on(codes_in, grad_in, codes_out, grad_out):
    codes_out[...] = codes_in[...]
    grad_out[...] = grad_in[...]


def local(devices, image, mask, dictionary, penalty):
    block_rows, columns, features = image.shape
    atoms = dictionary.shape[0]
    rows = block_rows * columns
    quads = devices // QUAD
    fused = devices % QUAD == 0 and features % (quads * 128) == 0 and features // devices % 16 == 0
    own = features // devices
    slots = (quads, own) if fused else (1, 16)
    dma, vmem = pltpu.SemaphoreType.DMA, pltpu.VMEM
    near, there = pl.BlockSpec(memory_space=pltpu.VMEM), pl.BlockSpec(memory_space=pl.ANY)
    codes, grad = pl.pallas_call(
        functools.partial(kernel, devices, block_rows, columns, fused),
        out_shape=(
            jax.ShapeDtypeStruct((block_rows, atoms, columns), F32),
            jax.ShapeDtypeStruct((own if fused else features, 4 * atoms), F32),
        ),
        in_specs=[there, near, there, near],
        out_specs=(near, near),
        scratch_shapes=[
            vmem((rows, atoms), F32),
            vmem((atoms, 4, features), BF16),
            vmem((rows, features), BF16),
            vmem((4 * atoms, features), BF16),
            vmem((rows, features), BF16),
            vmem((rows, features), BF16),
            vmem((rows, 128), F32),
            vmem((rows, 128), F32),
            vmem((2, columns // 2, 128), F32),
            vmem((2, columns // 2, 128), F32),
            vmem((2, rows, 128), BF16),
            vmem((2, columns, 128), BF16),
            vmem((slots[0], QUAD * slots[1], 4 * atoms), F32),
            vmem((slots[0], 2, slots[1], 4 * atoms), BF16),
            vmem((slots[0], 2, slots[1], 4 * atoms), BF16),
            vmem((slots[0], slots[1], 4 * atoms), BF16),
            vmem((slots[0], slots[1], 4 * atoms), BF16),
            vmem((slots[0], slots[1], 4 * atoms), BF16),
            vmem((slots[0], slots[1], 4 * atoms), BF16),
            dma((2,)), dma,
            dma((2,)), dma((2,)), dma((2,)), dma((2,)),
            dma((slots[0],)), dma((slots[0],)), dma((slots[0],)),
            dma((slots[0],)), dma((slots[0],)), dma((slots[0],)),
        ],
        compiler_params=pltpu.CompilerParams(
            collective_id=0, has_side_effects=True, vmem_limit_bytes=56 * 1024 * 1024
        ),
    )(image.reshape(rows, features), mask, dictionary, penalty.reshape(1, atoms))
    if not fused:
        grad = lax.psum_scatter(grad, "row", scatter_dimension=0, tiled=True)
    codes, grad = pl.pallas_call(
        hand_on,
        out_shape=(
            jax.ShapeDtypeStruct(codes.shape, F32),
            jax.ShapeDtypeStruct(grad.shape, F32),
        ),
        in_specs=[near, near],
        out_specs=(near, near),
    )(codes, grad)
    return (jnp.transpose(codes, (0, 2, 1)), grad)


def solution(mesh):
    return jax.shard_map(
        functools.partial(local, mesh.shape["row"]),
        mesh=mesh,
        in_specs=(P(("grp", "row"), None, None), P(("grp", "row"), None), P(), P()),
        out_specs=(P(("grp", "row"), None, None), P(("grp", "row"), None)),
        check_vma=False,
    )
```
